32 devices in a mesh: gx: 4 (over z), gy: 8 (over y, x, core).
Axes of the slice: x: 2, y: 2, z: 4, core: 2. Of those that a mesh axis runs over, the one named last changes fastest.
Arguments:
- velocity: float32 [2, 2048, 4096], P(None, 'gx', 'gy'), may hold values from -6 to 6
- observed: float32 [2, 2048, 4096], P(None, 'gx', 'gy'), may hold values from -6 to 6
- thickness: float32 [2048, 4096], P('gx', 'gy'), may hold values from 0.5 to 2
- rate_factor: float32 [2048, 4096], P('gx', 'gy'), may hold values from 0.5 to 2
- friction: float32 [2048, 4096], P('gx', 'gy'), may hold values from 0.1 to 10
- cell_mask: int32 [2048, 4096], P('gx', 'gy'), may hold values from 0 to 2
- front_codes: int32 [2048, 4096], P('gx', 'gy'), may hold values from 0 to 15
- modes_x: bfloat16 [2048, 512], P('gx'), may hold values from -0.125 to 0.125
- modes_y: bfloat16 [4096, 512], P('gy'), may hold values from -0.09375 to 0.09375
Outputs:
- adjoint: float32 [2, 2048, 4096], P(None, 'gx', 'gy')
- coefficients: float32 [512, 512], P('gx', 'gy')
The draws below stay inside these ranges and needn't reach their ends.
Inputs may be any that keep to these rules, and one draw needn't show every extreme that they name: `cell_mask`: 0 is ocean, 1 floating ice, 2 grounded ice. `front_codes`: bit 0, 1, 2, 3 marks a calving front on the cell's lower first-dimension, upper first-dimension, lower second-dimension, upper second-dimension face.
All inputs are finite; a program needn't handle non-finite values.
Results may differ from the reference program's by a relative error of at most 0.0029.
Values sent between devices are 32-bit elements; how exact they have to be, the bound alone decides.
A program may use at most 128 MiB of HBM per device.

```python
import math
import jax
import jax.numpy as jnp
from jax import lax

KM = 512
SWEEPS = 3
NX = 2048
NY = 4096


def place_ends(values, stream_key, smallest, high):
    spot = [jax.random.randint(jax.random.fold_in(stream_key, axis), (), 0, length) for axis, length in enumerate(values.shape)]
    longest = values.shape.index(max(values.shape))
    next_to = spot[:longest] + [(spot[longest] + 1) % values.shape[longest]] + spot[longest + 1:]
    return values.at[tuple(spot)].set(smallest).at[tuple(next_to)].set(high)


def level_of(stream_key, extent, shards, low, top_value):
    def one(axis_at, parts):
        heights = jax.random.uniform(jax.random.fold_in(jax.random.fold_in(stream_key, 6), axis_at), (parts,), jnp.float32, low / len(shards), top_value / len(shards))
        return jnp.repeat(jnp.exp(heights), extent[axis_at] // parts).reshape((-1,) + (1,) * (len(extent) - axis_at - 1))

    level = one(*shards[0])
    for cut in shards[1:]:
        level = level * one(*cut)
    return level


def centred(rng, extent, spread, limit, shards=(), kind=jnp.bfloat16):
    result = spread * jax.random.normal(rng, extent, jnp.float32)
    if shards:
        result = result * level_of(rng, extent, shards, -0.22, 0.18)
    return jnp.clip(result, -limit, limit).astype(kind)


def setup_inputs(seed: int = 0) -> dict:
    keys = jax.random.split(jax.random.key(seed), 10)
    return {
        "velocity": centred(keys[0], (2, NX, NY), 1.0, 6.0, ((1, 4), (2, 8)), jnp.float32),
        "observed": centred(keys[1], (2, NX, NY), 1.0, 6.0, ((1, 4), (2, 8)), jnp.float32),
        "thickness": jnp.clip(jnp.exp(math.log(2.0) - 1.3862944 * jax.random.uniform(keys[2], (NX, NY), jnp.float32) ** level_of(keys[2], (NX, NY), ((0, 4), (1, 8)), -0.2, 0.2)), 0.5, 2.0),
        "rate_factor": jnp.clip(jnp.exp(math.log(2.0) - 1.3862944 * jax.random.uniform(keys[3], (NX, NY), jnp.float32) ** level_of(keys[3], (NX, NY), ((0, 4), (1, 8)), -0.2, 0.2)), 0.5, 2.0),
        "friction": jnp.clip(jnp.exp(math.log(10.0) - 4.6051702 * jax.random.uniform(keys[4], (NX, NY), jnp.float32) ** level_of(keys[4], (NX, NY), ((0, 4), (1, 8)), -0.2, 0.2)), 0.1, 10.0),
        "cell_mask": place_ends(jax.random.randint(keys[5], (NX, NY), 0, 3), jax.random.fold_in(keys[5], 1), 0, 2).astype(jnp.int32),
        "front_codes": place_ends(jax.random.randint(keys[6], (NX, NY), 0, 16), jax.random.fold_in(keys[6], 1), 0, 15).astype(jnp.int32),
        "modes_x": centred(keys[7], (NX, KM), NX ** -0.5, 0.125, ((0, 4),)),
        "modes_y": centred(keys[8], (NY, KM), NY ** -0.5, 0.09375, ((0, 8),)),
    }


def viscosity(padded, stiffness):
    along_x = (padded[:, 2:, 1:-1] - padded[:, :-2, 1:-1]) * 0.5
    along_y = (padded[:, 1:-1, 2:] - padded[:, 1:-1, :-2]) * 0.5
    shear = along_y[0] + along_x[1]
    strain = along_x[0] * along_x[0] + along_y[1] * along_y[1] + along_x[0] * along_y[1] + 0.25 * shear * shear
    return stiffness * 0.5 * (strain + 0.01) ** (-1.0 / 3.0)

def face_terms(eta_pad):
    center = eta_pad[1:-1, 1:-1]
    lower_x = jnp.sqrt(center * eta_pad[:-2, 1:-1])
    upper_x = jnp.sqrt(center * eta_pad[2:, 1:-1])
    lower_y = jnp.sqrt(center * eta_pad[1:-1, :-2])
    upper_y = jnp.sqrt(center * eta_pad[1:-1, 2:])
    return (lower_x, upper_x, lower_y, upper_y)

def front_count(front_codes):
    total = jnp.zeros(front_codes.shape, jnp.float32)
    for bit_index in range(4):
        total = total + (jnp.right_shift(front_codes, bit_index) & 1).astype(jnp.float32)
    return total

def relax(adjoint_pad, faces, rhs, diagonal_sum):
    lower_x, upper_x, lower_y, upper_y = faces
    x_weights = jnp.array([4.0, 1.0], jnp.float32).reshape(2, 1, 1)
    y_weights = jnp.array([1.0, 4.0], jnp.float32).reshape(2, 1, 1)
    near_x = lower_x * adjoint_pad[:, :-2, 1:-1] + upper_x * adjoint_pad[:, 2:, 1:-1]
    near_y = lower_y * adjoint_pad[:, 1:-1, :-2] + upper_y * adjoint_pad[:, 1:-1, 2:]
    return (rhs + x_weights * near_x + y_weights * near_y) / diagonal_sum

def reference(velocity, observed, thickness, rate_factor, friction, cell_mask, front_codes, modes_x, modes_y):
    ice = (cell_mask >= 1).astype(jnp.float32)
    grounded = (cell_mask == 2).astype(jnp.float32)
    stiffness = thickness * ice * rate_factor
    vel_pad = jnp.pad(velocity, ((0, 0), (1, 1), (1, 1)))
    eta = viscosity(vel_pad, stiffness)
    eta_pad = jnp.pad(eta, ((1, 1), (1, 1)))
    faces = face_terms(eta_pad)
    lower_x, upper_x, lower_y, upper_y = faces
    x_weights = jnp.array([4.0, 1.0], jnp.float32).reshape(2, 1, 1)
    y_weights = jnp.array([1.0, 4.0], jnp.float32).reshape(2, 1, 1)
    extra = 2.0 * eta * front_count(front_codes) + friction * grounded + 1.0
    diagonal_sum = x_weights * (lower_x + upper_x) + y_weights * (lower_y + upper_y) + extra
    rhs = ice * (velocity - observed)
    adjoint = rhs / diagonal_sum
    for sweep in range(SWEEPS - 1):
        adjoint_pad = jnp.pad(adjoint, ((0, 0), (1, 1), (1, 1)))
        adjoint = relax(adjoint_pad, faces, rhs, diagonal_sum)
    gradient = (-(friction * grounded) * (velocity[0] * adjoint[0] + velocity[1] * adjoint[1])).astype(jnp.bfloat16)
    partial_rows = lax.dot_general(modes_x, gradient, (((0,), (0,)), ((), ())), preferred_element_type=jnp.float32)
    coefficients = jnp.dot(partial_rows, modes_y.astype(jnp.float32), precision=lax.Precision.HIGHEST)
    return (adjoint, coefficients)
```

```python
import functools

import jax
import jax.numpy as jnp
from jax import lax
from jax.experimental import pallas as pl
from jax.experimental.pallas import tpu as pltpu
from jax.sharding import PartitionSpec as P

SWEEPS = 3
ROWS = 16
LT = 128
MESH = pl.DeviceIdType.MESH
F32 = jnp.float32
BF16 = jnp.bfloat16


def ew_shift(block, width):
    left = pltpu.roll(block, 1, 1)[:, LT : LT + width]
    right = pltpu.roll(block, block.shape[1] - 1, 1)[:, LT : LT + width]
    return left, right


def ns_shift(block, rows):
    up = pltpu.roll(block, 1, 0)[8 : 8 + rows]
    down = pltpu.roll(block, block.shape[0] - 1, 0)[8 : 8 + rows]
    return up, down


def kernel(
    ngx, ngy,
    vel_h, obs_h, thick_h, rate_h, fric_h, mask_h, codes_h, mx_h, my_h,
    adj_h, coef_ref,
    vel, obs, thick, rate, fric, mask, codes, mx, my,
    s_pad, q1, q2, p_f, g_f, e_f, adj, grad, mxt, myt, t_hi, t_lo,
    edge_out, edge_in, r_send, r_acc, r_in, half_in, z_out, z_in,
    load_sem, store_sem, halo_send, halo_recv, col_send, col_recv,
    pair_sem, half_send, half_recv, z_send, z_recv,
):
    h, w = thick.shape
    ix, iy = lax.axis_index("gx"), lax.axis_index("gy")
    mid = pl.ds(LT, w)
    body = pl.ds(8, h)

    loads = [
        pltpu.make_async_copy(vel_h, vel.at[:, body, mid], load_sem.at[0]),
        pltpu.make_async_copy(mx_h, mx, load_sem.at[1]),
        pltpu.make_async_copy(my_h, my, load_sem.at[2]),
        pltpu.make_async_copy(thick_h, thick, load_sem.at[3]),
        pltpu.make_async_copy(rate_h, rate, load_sem.at[4]),
        pltpu.make_async_copy(mask_h, mask, load_sem.at[5]),
        pltpu.make_async_copy(fric_h, fric, load_sem.at[6]),
        pltpu.make_async_copy(codes_h, codes, load_sem.at[7]),
        pltpu.make_async_copy(obs_h, obs, load_sem.at[8]),
    ]
    for load in loads:
        load.start()

    barrier = pltpu.get_barrier_semaphore()
    for off in range(1, ngx):
        pl.semaphore_signal(barrier, inc=1, device_id=(lax.rem(ix + off, ngx), iy), device_id_type=MESH)
    for off in range(1, ngy):
        pl.semaphore_signal(barrier, inc=1, device_id=(ix, lax.rem(iy + off, ngy)), device_id_type=MESH)
    pl.semaphore_wait(barrier, ngx - 1 + ngy - 1)

    has_n, has_s, has_w, has_e = ix > 0, ix < ngx - 1, iy > 0, iy < ngy - 1

    def row_copies(k, ref):
        down = pltpu.make_async_remote_copy(
            ref.at[:, pl.ds(h, 8), mid], ref.at[:, pl.ds(0, 8), mid],
            halo_send.at[k, 0], halo_recv.at[k, 0], device_id=(ix + 1, iy), device_id_type=MESH)
        up = pltpu.make_async_remote_copy(
            ref.at[:, pl.ds(8, 8), mid], ref.at[:, pl.ds(h + 8, 8), mid],
            halo_send.at[k, 1], halo_recv.at[k, 1], device_id=(ix - 1, iy), device_id_type=MESH)
        return down, up

    def col_copies(k, n):
        east = pltpu.make_async_remote_copy(
            edge_out.at[k, 0, pl.ds(0, n)], edge_in.at[k, 0, pl.ds(0, n)],
            col_send.at[k, 0], col_recv.at[k, 0], device_id=(ix, iy + 1), device_id_type=MESH)
        west = pltpu.make_async_remote_copy(
            edge_out.at[k, 1, pl.ds(0, n)], edge_in.at[k, 1, pl.ds(0, n)],
            col_send.at[k, 1], col_recv.at[k, 1], device_id=(ix, iy - 1), device_id_type=MESH)
        return east, west

    def send_edges(k, ref):
        n = ref.shape[0]
        down, up = row_copies(k, ref)
        east, west = col_copies(k, n)

        @pl.when(has_s)
        def _():
            down.start()

        @pl.when(has_n)
        def _():
            up.start()

        for c in range(n):
            edge_out[k, 0, c] = ref[c, body, pl.ds(w, LT)].T[LT - 8 :]
            edge_out[k, 1, c] = ref[c, body, pl.ds(LT, LT)].T[:8]

        @pl.when(has_e)
        def _():
            east.start()

        @pl.when(has_w)
        def _():
            west.start()

    def take_edges(k, ref):
        n = ref.shape[0]
        down, up = row_copies(k, ref)
        east, west = col_copies(k, n)

        @pl.when(has_w)
        def _():
            east.wait_recv()
            for c in range(n):
                ref[c, body, pl.ds(0, LT)] = jnp.broadcast_to(edge_in[k, 0, c][7:8], (LT, h)).T

        @pl.when(iy == 0)
        def _():
            ref[:, body, pl.ds(0, LT)] = jnp.zeros((n, h, LT), F32)

        @pl.when(has_e)
        def _():
            west.wait_recv()
            for c in range(n):
                ref[c, body, pl.ds(LT + w, LT)] = jnp.broadcast_to(edge_in[k, 1, c][0:1], (LT, h)).T

        @pl.when(iy == ngy - 1)
        def _():
            ref[:, body, pl.ds(LT + w, LT)] = jnp.zeros((n, h, LT), F32)

        @pl.when(has_n)
        def _():
            down.wait_recv()

        @pl.when(ix == 0)
        def _():
            ref[:, pl.ds(0, 8), mid] = jnp.zeros((n, 8, w), F32)

        @pl.when(has_s)
        def _():
            up.wait_recv()

        @pl.when(ix == ngx - 1)
        def _():
            ref[:, pl.ds(h + 8, 8), mid] = jnp.zeros((n, 8, w), F32)

    def drain_edges(k, ref):
        n = ref.shape[0]
        down, up = row_copies(k, ref)
        east, west = col_copies(k, n)
        for there, copy in ((has_s, down), (has_n, up), (has_e, east), (has_w, west)):

            @pl.when(there)
            def _(copy=copy):
                copy.wait_send()

    def over_rows(step):
        def one(i, carry):
            step(pl.multiple_of(i * ROWS, ROWS))
            return carry

        lax.fori_loop(0, h // ROWS, one, 0)

    def neighbours(ref, c, r):
        up, down = ns_shift(ref[c, pl.ds(r, ROWS + 16), mid], ROWS)
        left, right = ew_shift(ref[c, pl.ds(r + 8, ROWS), :], w)
        return up, down, left, right

    loads[0].wait()
    send_edges(0, vel)
    loads[1].wait()
    loads[2].wait()
    mxt[...] = mx[...].T
    myt[...] = my[...].T.reshape(myt.shape)
    for load in loads[3:6]:
        load.wait()
    take_edges(0, vel)

    def viscosity(r):
        up, down, left, right = neighbours(vel, 0, r)
        ux, uy = down - up, right - left
        up, down, left, right = neighbours(vel, 1, r)
        vx, vy = down - up, right - left
        shear = uy + vx
        strain = 0.25 * (ux * ux + vy * vy + ux * vy + 0.25 * (shear * shear))
        here = pl.ds(r, ROWS)
        half = 0.5 * thick[here, :] * rate[here, :]
        root = half * lax.rsqrt(half) * jnp.exp2(jnp.log2(strain + 0.01) * (-1.0 / 6.0))
        s_pad[0, pl.ds(r + 8, ROWS), mid] = jnp.where(mask[here, :] >= 1, root, 0.0)

    over_rows(viscosity)
    send_edges(1, s_pad)
    for load in loads[6:]:
        load.wait()

    def sources(r):
        here, there = pl.ds(r, ROWS), pl.ds(r + 8, ROWS)
        kind = mask[here, :]
        s = s_pad[0, there, mid]
        drag = jnp.where(kind == 2, fric[here, :], 0.0)
        fric[here, :] = drag
        code = codes[here, :] & 15
        pairs = code - (lax.shift_right_logical(code, 1) & 5)
        fronts = ((pairs & 3) + lax.shift_right_logical(pairs, 2)).astype(F32)
        e_f[here, :] = 2.0 * (s * s) * fronts + drag + 1.0
        for c in range(2):
            obs[c, here, :] = jnp.where(kind >= 1, vel[c, there, mid] - obs[c, here, :], 0.0)

    over_rows(sources)
    take_edges(1, s_pad)

    def first(r):
        here, there = pl.ds(r, ROWS), pl.ds(r + 8, ROWS)
        up, down, left, right = neighbours(s_pad, 0, r)
        ns, ew = up + down, left + right
        s = s_pad[0, there, mid]
        e = e_f[here, :]
        for c, total in ((0, 4.0 * ns + ew), (1, ns + 4.0 * ew)):
            inverse = 1.0 / (s * total + e)
            value = obs[c, here, :] * inverse
            p_f[c, here, :] = value
            g_f[c, here, :] = s * inverse
            q1[c, there, mid] = s * value

    over_rows(first)
    send_edges(2, q1)
    take_edges(2, q1)

    def weighted(ref, c, r):
        up, down, left, right = neighbours(ref, c, r)
        ns, ew = up + down, left + right
        return 4.0 * ns + ew if c == 0 else ns + 4.0 * ew

    def second(r):
        here, there = pl.ds(r, ROWS), pl.ds(r + 8, ROWS)
        s = s_pad[0, there, mid]
        for c in range(2):
            total = weighted(q1, c, r)
            q2[c, there, mid] = q1[c, there, mid] + s * g_f[c, here, :] * total

    over_rows(second)
    send_edges(3, q2)
    take_edges(3, q2)

    def third(r):
        here, there = pl.ds(r, ROWS), pl.ds(r + 8, ROWS)
        flux = None
        for c in range(2):
            value = p_f[c, here, :] + g_f[c, here, :] * weighted(q2, c, r)
            adj[c, here, :] = value
            term = vel[c, there, mid] * value
            flux = term if flux is None else flux + term
        grad[here, :] = (-fric[here, :] * flux).astype(BF16)

    over_rows(third)
    store = pltpu.make_async_copy(adj, adj_h, store_sem)
    store.start()

    table = jnp.dot(mxt[...], grad[...], preferred_element_type=F32)
    high = table.astype(BF16)
    t_hi[...] = high
    t_lo[...] = (table - high.astype(F32)).astype(BF16)

    nblk, kb, km = r_acc.shape
    core = lax.rem(iy, 2)

    def project(side):
        rows = myt[:, side].reshape(nblk * kb, h)
        dims = (((1,), (1,)), ((), ()))
        out = lax.dot_general(rows, t_hi[...], dims, preferred_element_type=F32)
        out = out + lax.dot_general(rows, t_lo[...], dims, preferred_element_type=F32)
        return out.reshape(nblk, kb, km)

    r_send[...] = project(1 - core)
    pair = pltpu.make_async_remote_copy(
        r_send, r_in, pair_sem.at[0], pair_sem.at[1],
        device_id=(ix, iy + 1 - 2 * core), device_id_type=MESH)
    pair.start()
    r_acc[...] = project(core)
    pair.wait_recv()
    r_acc[...] += r_in[...]

    nbits = nblk.bit_length() - 1
    hw = km // 2
    cell = iy // 2
    bits = [lax.rem(cell // (1 << t), 2) for t in range(nbits)]
    sent = []
    live = [dict(), dict()]
    slot = 0
    for stage in range(nbits):
        flying = []
        for half in range(2):
            t = stage if half == 0 else nbits - 1 - stage
            free = [b for b in range(nbits) if b not in live[half] and b != t]
            lanes = pl.ds(half * hw, hw)
            for combo in range(1 << len(free)):
                fixed = sum(((combo >> n) & 1) << b for n, b in enumerate(free))
                fixed = fixed + sum((bits[b] * (1 << b) for b in live[half]), 0)
                src = fixed + (1 - bits[t]) * (1 << t)
                dst = fixed + bits[t] * (1 << t)
                copy = pltpu.make_async_remote_copy(
                    r_acc.at[src, :, lanes], half_in.at[slot],
                    half_send.at[slot], half_recv.at[slot],
                    device_id=(ix, iy + (1 - 2 * bits[t]) * (2 << t)), device_id_type=MESH)
                copy.start()
                flying.append((copy, dst, lanes, slot))
                slot += 1
            live[half][t] = True
        for copy, dst, lanes, place in flying:
            copy.wait_recv()
            r_acc[dst, :, lanes] += half_in[place]
            sent.append(copy)

    ab = km // ngx
    for d in range(ngx):
        z_out[d] = r_acc[cell, :, d * ab : (d + 1) * ab]
    copies = []
    for off in range(1, ngx):
        to = lax.rem(ix + off, ngx)
        copy = pltpu.make_async_remote_copy(
            z_out.at[to], z_in.at[off - 1], z_send.at[off - 1], z_recv.at[off - 1],
            device_id=(to, iy), device_id_type=MESH)
        copy.start()
        copies.append(copy)
    total = z_out[ix]
    for off, copy in enumerate(copies):
        copy.wait_recv()
        total = total + z_in[off]
    coef_ref[...] = total.T

    for copy in copies + sent + [pair]:
        copy.wait_send()
    for k, ref in enumerate((vel, s_pad, q1, q2)):
        drain_edges(k, ref)
    store.wait()


def shards(ngx, ngy, velocity, observed, thickness, rate_factor, friction, cell_mask, front_codes, modes_x, modes_y):
    h, w = thickness.shape
    km = modes_x.shape[1]
    nblk, kb, ab = ngy // 2, km // ngy, km // ngx
    slots = 2 * sum(nblk >> (t + 1) for t in range(nblk.bit_length() - 1))
    any_spec = pl.BlockSpec(memory_space=pl.ANY)
    pad = (h + 16, w + 2 * LT)
    dma = pltpu.SemaphoreType.DMA
    return pl.pallas_call(
        functools.partial(kernel, ngx, ngy),
        out_shape=(
            jax.ShapeDtypeStruct((2, h, w), F32),
            jax.ShapeDtypeStruct((ab, kb), F32),
        ),
        in_specs=[any_spec] * 9,
        out_specs=(any_spec, pl.BlockSpec(memory_space=pltpu.VMEM)),
        scratch_shapes=[
            pltpu.VMEM((2, *pad), F32),
            pltpu.VMEM((2, h, w), F32),
            pltpu.VMEM((h, w), F32),
            pltpu.VMEM((h, w), F32),
            pltpu.VMEM((h, w), F32),
            pltpu.VMEM((h, w), jnp.int32),
            pltpu.VMEM((h, w), jnp.int32),
            pltpu.VMEM((h, km), BF16),
            pltpu.VMEM((w, km), BF16),
            pltpu.VMEM((1, *pad), F32),
            pltpu.VMEM((2, *pad), F32),
            pltpu.VMEM((2, *pad), F32),
            pltpu.VMEM((2, h, w), F32),
            pltpu.VMEM((2, h, w), F32),
            pltpu.VMEM((h, w), F32),
            pltpu.VMEM((2, h, w), F32),
            pltpu.VMEM((h, w), BF16),
            pltpu.VMEM((km, h), BF16),
            pltpu.VMEM((nblk, 2, kb, w), BF16),
            pltpu.VMEM((km, w), BF16),
            pltpu.VMEM((km, w), BF16),
            pltpu.VMEM((4, 2, 2, 8, h), F32),
            pltpu.VMEM((4, 2, 2, 8, h), F32),
            pltpu.VMEM((nblk, kb, km), F32),
            pltpu.VMEM((nblk, kb, km), F32),
            pltpu.VMEM((nblk, kb, km), F32),
            pltpu.VMEM((slots, kb, km // 2), F32),
            pltpu.VMEM((ngx, kb, ab), F32),
            pltpu.VMEM((ngx - 1, kb, ab), F32),
            dma((9,)),
            dma,
            dma((4, 2)),
            dma((4, 2)),
            dma((4, 2)),
            dma((4, 2)),
            dma((2,)),
            dma((slots,)),
            dma((slots,)),
            dma((ngx - 1,)),
            dma((ngx - 1,)),
        ],
        compiler_params=pltpu.CompilerParams(
            collective_id=0, has_side_effects=True, vmem_limit_bytes=56 * 1024 * 1024
        ),
    )(velocity, observed, thickness, rate_factor, friction, cell_mask, front_codes, modes_x, modes_y)


def solution(mesh):
    tile = P("gx", "gy")
    pair = P(None, "gx", "gy")
    return jax.shard_map(
        functools.partial(shards, mesh.shape["gx"], mesh.shape["gy"]),
        mesh=mesh,
        in_specs=(pair, pair, tile, tile, tile, tile, tile, P("gx", None), P("gy", None)),
        out_specs=(pair, tile),
        check_vma=False,
    )
```

```python
import functools

import jax
import jax.numpy as jnp
from jax import lax
from jax.experimental import pallas as pl
from jax.experimental.pallas import tpu as pltpu
from jax.sharding import PartitionSpec as P

SWEEPS = 3
ROWS = 32
LT = 128
VMEM_LIMIT = 48 * 1024 * 1024
MESH = pl.DeviceIdType.MESH
F32 = jnp.float32
BF16 = jnp.bfloat16


def kernel(
    ngx, ngy,
    vel_h, obs_h, thick_h, rate_h, fric_h, mask_h, codes_h, mx_h, my_h,
    adj, coef_ref,
    vel, obs, thick, rate, fric, mask, codes, mx, my,
    s_pad, q1, q2, p_f, g_f, e_f, grad, mxt, myt, t_hi, t_lo,
    edge_out, edge_in, halo, r_send, r_acc, r_in, half_in, z_out, z_in,
    vel_sem, load_sem, halo_send, halo_recv, col_send, col_recv,
    pair_sem, half_send, half_recv, z_send, z_recv,
):
    h, w = thick.shape
    nt = w // LT
    ix, iy = lax.axis_index("gx"), lax.axis_index("gy")
    body = pl.ds(8, h)
    outer, inner = (0, nt - 1), tuple(range(1, nt - 1))

    vel_loads = [
        pltpu.make_async_copy(
            vel_h.at[:, :, pl.ds(t * LT, LT)], vel.at[:, t, body], vel_sem.at[t])
        for t in outer + inner
    ]
    loads = [
        pltpu.make_async_copy(thick_h, thick, load_sem.at[0]),
        pltpu.make_async_copy(rate_h, rate, load_sem.at[1]),
        pltpu.make_async_copy(mask_h, mask, load_sem.at[2]),
        pltpu.make_async_copy(fric_h, fric, load_sem.at[3]),
        pltpu.make_async_copy(codes_h, codes, load_sem.at[4]),
        pltpu.make_async_copy(obs_h, obs, load_sem.at[5]),
        pltpu.make_async_copy(mx_h, mx, load_sem.at[6]),
        pltpu.make_async_copy(my_h, my, load_sem.at[7]),
    ]
    for load in vel_loads + loads:
        load.start()

    barrier = pltpu.get_barrier_semaphore()
    for off in range(1, ngx):
        pl.semaphore_signal(barrier, inc=1, device_id=(lax.rem(ix + off, ngx), iy), device_id_type=MESH)
    for off in range(1, ngy):
        pl.semaphore_signal(barrier, inc=1, device_id=(ix, lax.rem(iy + off, ngy)), device_id_type=MESH)
    pl.semaphore_wait(barrier, ngx - 1 + ngy - 1)

    has_n, has_s, has_w, has_e = ix > 0, ix < ngx - 1, iy > 0, iy < ngy - 1

    fields = (vel, s_pad, q1, q2)

    for missing, rows in ((ix == 0, 0), (ix == ngx - 1, h + 8)):

        @pl.when(missing)
        def _(rows=rows):
            for ref in fields:
                ref[:, :, pl.ds(rows, 8)] = jnp.zeros((ref.shape[0], nt, 8, LT), F32)

    for missing, side in ((iy == 0, 0), (iy == ngy - 1, 1)):

        @pl.when(missing)
        def _(side=side):
            edge_in[:, side] = jnp.zeros((4, 8, h), F32)

    def copies_of(k):
        ref = fields[k]
        down = pltpu.make_async_remote_copy(
            ref.at[:, :, pl.ds(h, 8)], ref.at[:, :, pl.ds(0, 8)],
            halo_send.at[k, 0], halo_recv.at[k, 0], device_id=(ix + 1, iy), device_id_type=MESH)
        up = pltpu.make_async_remote_copy(
            ref.at[:, :, pl.ds(8, 8)], ref.at[:, :, pl.ds(h + 8, 8)],
            halo_send.at[k, 1], halo_recv.at[k, 1], device_id=(ix - 1, iy), device_id_type=MESH)
        east = pltpu.make_async_remote_copy(
            edge_out.at[k], edge_in.at[k, 0],
            col_send.at[k, 0], col_recv.at[k, 0], device_id=(ix, iy + 1), device_id_type=MESH)
        west = pltpu.make_async_remote_copy(
            edge_out.at[k], edge_in.at[k, 1],
            col_send.at[k, 1], col_recv.at[k, 1], device_id=(ix, iy - 1), device_id_type=MESH)
        return (has_s, down), (has_n, up), (has_e, east), (has_w, west)

    def start(there, copy):
        @pl.when(there)
        def _():
            copy.start()

    def send_rows(k):
        for there, copy in copies_of(k)[:2]:
            start(there, copy)

    def send_columns(k):
        ref = fields[k]
        lane = lax.broadcasted_iota(jnp.int32, (h, LT), 1)
        pack = pltpu.roll(ref[0, nt - 1, body], 1, 1)
        pack = jnp.where(lane == 7, pltpu.roll(ref[0, 0, body], 7, 1), pack)
        if ref.shape[0] == 2:
            pack = jnp.where(lane == 1, pltpu.roll(ref[1, nt - 1, body], 2, 1), pack)
            pack = jnp.where(lane == 6, pltpu.roll(ref[1, 0, body], 6, 1), pack)
        edge_out[k] = pack.T[:8]
        for there, copy in copies_of(k)[2:]:
            start(there, copy)

    def take_edges(k):
        (_, down), (_, up), (_, east), (_, west) = copies_of(k)
        for there, copy in ((has_w, east), (has_e, west), (has_n, down), (has_s, up)):

            @pl.when(there)
            def _(copy=copy):
                copy.wait_recv()

        row = lax.broadcasted_iota(jnp.int32, (8, h), 0)
        both = jnp.where(row < 4, edge_in[k, 0], edge_in[k, 1])
        halo[k] = jnp.concatenate([both] * (LT // 8), axis=0).T

    def drain_edges(k):
        for there, copy in copies_of(k):

            @pl.when(there)
            def _(copy=copy):
                copy.wait_send()

    def rows_of(step, first, last, stride=ROWS):
        def one(i, carry):
            step(pl.multiple_of(first + i * stride, ROWS))
            return carry

        lax.fori_loop(0, (last - first) // stride, one, 0)

    def border(step):
        rows_of(lambda r: step(r, outer), 0, h)
        rows_of(lambda r: step(r, inner), 0, 2 * (h - ROWS), h - ROWS)

    def interior(step):
        rows_of(lambda r: step(r, inner), ROWS, h - ROWS)

    lanes = lax.broadcasted_iota(jnp.int32, (ROWS, LT), 1)
    at_first, at_last = lanes == 0, lanes == LT - 1

    def cols(t):
        return pl.ds(t * LT, LT)

    def neighbours(k, c, r, t, kept):
        ref = fields[k]

        def turned(tile, by):
            if (c, tile, by) not in kept:
                kept[c, tile, by] = pltpu.roll(ref[c, tile, pl.ds(r + 8, ROWS)], by, 1)
            return kept[c, tile, by]

        def edge(by):
            value = halo[k, pl.ds(r, ROWS)]
            return pltpu.roll(value, by, 1) if c else value

        up = ref[c, t, pl.ds(r + 7, ROWS)]
        down = ref[c, t, pl.ds(r + 9, ROWS)]
        before = turned(t - 1, 1) if t else edge(LT - 1)
        after = turned(t + 1, LT - 1) if t < nt - 1 else edge(1)
        left = jnp.where(at_first, before, turned(t, 1))
        right = jnp.where(at_last, after, turned(t, LT - 1))
        return up, down, left, right

    def weighted(k, c, r, t, kept):
        up, down, left, right = neighbours(k, c, r, t, kept)
        ns, ew = up + down, left + right
        return 4.0 * ns + ew if c == 0 else ns + 4.0 * ew

    def viscosity(r, tiles):
        kept = {}
        for t in tiles:
            up, down, left, right = neighbours(0, 0, r, t, kept)
            ux, uy = down - up, right - left
            up, down, left, right = neighbours(0, 1, r, t, kept)
            vx, vy = down - up, right - left
            shear = uy + vx
            strain = 0.25 * (ux * ux + vy * vy + ux * vy + 0.25 * (shear * shear))
            here = pl.ds(r, ROWS)
            half = 0.5 * thick[here, cols(t)] * rate[here, cols(t)]
            root = half * lax.rsqrt(half) * jnp.exp2(jnp.log2(strain + 0.01) * (-1.0 / 6.0))
            s_pad[0, t, pl.ds(r + 8, ROWS)] = jnp.where(mask[here, cols(t)] >= 1, root, 0.0)

    def sources(r, tiles):
        here, there = pl.ds(r, ROWS), pl.ds(r + 8, ROWS)
        for t in tiles:
            kind = mask[here, cols(t)]
            s = s_pad[0, t, there]
            drag = jnp.where(kind == 2, fric[here, cols(t)], 0.0)
            fric[here, cols(t)] = drag
            code = codes[here, cols(t)] & 15
            pairs = code - (lax.shift_right_logical(code, 1) & 5)
            fronts = ((pairs & 3) + lax.shift_right_logical(pairs, 2)).astype(F32)
            e_f[here, cols(t)] = 2.0 * (s * s) * fronts + drag + 1.0
            for c in range(2):
                obs[c, here, cols(t)] = jnp.where(kind >= 1, vel[c, t, there] - obs[c, here, cols(t)], 0.0)

    def first(r, tiles):
        here, there = pl.ds(r, ROWS), pl.ds(r + 8, ROWS)
        kept = {}
        for t in tiles:
            up, down, left, right = neighbours(1, 0, r, t, kept)
            ns, ew = up + down, left + right
            s = s_pad[0, t, there]
            e = e_f[here, cols(t)]
            for c, total in ((0, 4.0 * ns + ew), (1, ns + 4.0 * ew)):
                inverse = 1.0 / (s * total + e)
                value = obs[c, here, cols(t)] * inverse
                p_f[c, here, cols(t)] = value
                g_f[c, here, cols(t)] = s * inverse
                q1[c, t, there] = s * value

    def second(r, tiles):
        here, there = pl.ds(r, ROWS), pl.ds(r + 8, ROWS)
        kept = {}
        for t in tiles:
            s = s_pad[0, t, there]
            for c in range(2):
                total = weighted(2, c, r, t, kept)
                q2[c, t, there] = q1[c, t, there] + s * g_f[c, here, cols(t)] * total

    def third(r, tiles):
        here, there = pl.ds(r, ROWS), pl.ds(r + 8, ROWS)
        kept = {}
        for t in tiles:
            flux = None
            for c in range(2):
                value = p_f[c, here, cols(t)] + g_f[c, here, cols(t)] * weighted(3, c, r, t, kept)
                adj[c, here, cols(t)] = value
                term = vel[c, t, there] * value
                flux = term if flux is None else flux + term
            grad[here, cols(t)] = (-fric[here, cols(t)] * flux).astype(BF16)

    for load in vel_loads:
        load.wait()
    send_rows(0)
    send_columns(0)
    for load in loads[:3]:
        load.wait()
    take_edges(0)
    border(viscosity)
    send_columns(1)
    send_rows(1)
    interior(viscosity)
    for load in loads[3:]:
        load.wait()
    rows_of(lambda r: sources(r, range(nt)), 0, h)
    mxt[...] = mx[...].T
    myt[...] = my[...].T.reshape(myt.shape)
    take_edges(1)
    border(first)
    send_columns(2)
    send_rows(2)
    interior(first)
    take_edges(2)
    border(second)
    send_columns(3)
    send_rows(3)
    interior(second)
    interior(third)
    take_edges(3)
    border(third)

    table = jnp.dot(mxt[...], grad[...], preferred_element_type=F32)
    high = table.astype(BF16)
    t_hi[...] = high
    t_lo[...] = (table - high.astype(F32)).astype(BF16)

    nblk, kb, km = r_acc.shape
    core = lax.rem(iy, 2)

    def project(side):
        rows = myt[:, side].reshape(nblk * kb, h)
        dims = (((1,), (1,)), ((), ()))
        out = lax.dot_general(rows, t_hi[...], dims, preferred_element_type=F32)
        out = out + lax.dot_general(rows, t_lo[...], dims, preferred_element_type=F32)
        return out.reshape(nblk, kb, km)

    r_send[...] = project(1 - core)
    pair = pltpu.make_async_remote_copy(
        r_send, r_in, pair_sem.at[0], pair_sem.at[1],
        device_id=(ix, iy + 1 - 2 * core), device_id_type=MESH)
    pair.start()
    r_acc[...] = project(core)
    pair.wait_recv()
    r_acc[...] += r_in[...]

    nbits = nblk.bit_length() - 1
    hw = km // 2
    cell = iy // 2
    bits = [lax.rem(cell // (1 << t), 2) for t in range(nbits)]
    sent = []
    live = [dict(), dict()]
    slot = 0
    for stage in range(nbits):
        flying = []
        for half in range(2):
            t = stage if half == 0 else nbits - 1 - stage
            free = [b for b in range(nbits) if b not in live[half] and b != t]
            lanes = pl.ds(half * hw, hw)
            for combo in range(1 << len(free)):
                fixed = sum(((combo >> n) & 1) << b for n, b in enumerate(free))
                fixed = fixed + sum((bits[b] * (1 << b) for b in live[half]), 0)
                src = fixed + (1 - bits[t]) * (1 << t)
                dst = fixed + bits[t] * (1 << t)
                copy = pltpu.make_async_remote_copy(
                    r_acc.at[src, :, lanes], half_in.at[slot],
                    half_send.at[slot], half_recv.at[slot],
                    device_id=(ix, iy + (1 - 2 * bits[t]) * (2 << t)), device_id_type=MESH)
                copy.start()
                flying.append((copy, dst, lanes, slot))
                slot += 1
            live[half][t] = True
        for copy, dst, lanes, place in flying:
            copy.wait_recv()
            r_acc[dst, :, lanes] += half_in[place]
            sent.append(copy)

    ab = km // ngx
    for d in range(ngx):
        z_out[d] = r_acc[cell, :, d * ab : (d + 1) * ab]
    copies = []
    for off in range(1, ngx):
        to = lax.rem(ix + off, ngx)
        copy = pltpu.make_async_remote_copy(
            z_out.at[to], z_in.at[off - 1], z_send.at[off - 1], z_recv.at[off - 1],
            device_id=(to, iy), device_id_type=MESH)
        copy.start()
        copies.append(copy)
    total = z_out[ix]
    for off, copy in enumerate(copies):
        copy.wait_recv()
        total = total + z_in[off]
    coef_ref[...] = total

    for copy in copies + sent + [pair]:
        copy.wait_send()
    for k in range(4):
        drain_edges(k)


def write_results(adj, coef, adj_h, coef_h, adj_sem, coef_sem):
    rows = adj.shape[1] // 2
    copies = [pltpu.make_async_copy(coef, coef_h, coef_sem)]
    for n in range(4):
        part = (n % 2, pl.ds(n // 2 * rows, rows))
        copies.append(pltpu.make_async_copy(adj.at[part], adj_h.at[part], adj_sem.at[n]))
    for copy in copies:
        copy.start()
    for copy in copies:
        copy.wait()


def shards(ngx, ngy, velocity, observed, thickness, rate_factor, friction, cell_mask, front_codes, modes_x, modes_y):
    h, w = thickness.shape
    km = modes_x.shape[1]
    nblk, kb, ab = ngy // 2, km // ngy, km // ngx
    slots = 2 * sum(nblk >> (t + 1) for t in range(nblk.bit_length() - 1))
    hbm_spec = pl.BlockSpec(memory_space=pltpu.HBM)
    vmem_spec = pl.BlockSpec(memory_space=pltpu.VMEM)
    pad = (w // LT, h + 16, LT)
    dma = pltpu.SemaphoreType.DMA
    args = (velocity, observed, thickness, rate_factor, friction, cell_mask, front_codes, modes_x, modes_y)
    args = [pltpu.with_memory_space_constraint(x, pltpu.HBM) for x in args]
    adjoint, coefficients = pl.pallas_call(
        functools.partial(kernel, ngx, ngy),
        out_shape=(pltpu.VMEM((2, h, w), F32), pltpu.VMEM((kb, ab), F32)),
        in_specs=[hbm_spec] * 9,
        out_specs=(vmem_spec, vmem_spec),
        scratch_shapes=[
            pltpu.VMEM((2, *pad), F32),
            pltpu.VMEM((2, h, w), F32),
            pltpu.VMEM((h, w), F32),
            pltpu.VMEM((h, w), F32),
            pltpu.VMEM((h, w), F32),
            pltpu.VMEM((h, w), jnp.int32),
            pltpu.VMEM((h, w), jnp.int32),
            pltpu.VMEM((h, km), BF16),
            pltpu.VMEM((w, km), BF16),
            pltpu.VMEM((1, *pad), F32),
            pltpu.VMEM((2, *pad), F32),
            pltpu.VMEM((2, *pad), F32),
            pltpu.VMEM((2, h, w), F32),
            pltpu.VMEM((2, h, w), F32),
            pltpu.VMEM((h, w), F32),
            pltpu.VMEM((h, w), BF16),
            pltpu.VMEM((km, h), BF16),
            pltpu.VMEM((nblk, 2, kb, w), BF16),
            pltpu.VMEM((km, w), BF16),
            pltpu.VMEM((km, w), BF16),
            pltpu.VMEM((4, 8, h), F32),
            pltpu.VMEM((4, 2, 8, h), F32),
            pltpu.VMEM((4, h, LT), F32),
            pltpu.VMEM((nblk, kb, km), F32),
            pltpu.VMEM((nblk, kb, km), F32),
            pltpu.VMEM((nblk, kb, km), F32),
            pltpu.VMEM((slots, kb, km // 2), F32),
            pltpu.VMEM((ngx, kb, ab), F32),
            pltpu.VMEM((ngx - 1, kb, ab), F32),
            dma((w // LT,)),
            dma((8,)),
            dma((4, 2)),
            dma((4, 2)),
            dma((4, 2)),
            dma((4, 2)),
            dma((2,)),
            dma((slots,)),
            dma((slots,)),
            dma((ngx - 1,)),
            dma((ngx - 1,)),
        ],
        compiler_params=pltpu.CompilerParams(
            collective_id=0, has_side_effects=True, vmem_limit_bytes=VMEM_LIMIT
        ),
    )(*args)
    adjoint = pltpu.with_memory_space_constraint(adjoint, pltpu.VMEM)
    coefficients = pltpu.with_memory_space_constraint(coefficients, pltpu.VMEM)
    adjoint, coefficients = pl.pallas_call(
        write_results,
        out_shape=(
            jax.ShapeDtypeStruct((2, h, w), F32),
            jax.ShapeDtypeStruct((kb, ab), F32),
        ),
        in_specs=[vmem_spec, vmem_spec],
        out_specs=(hbm_spec, hbm_spec),
        scratch_shapes=[dma((4,)), dma],
    )(adjoint, coefficients)
    return adjoint, coefficients.T


def solution(mesh):
    tile = P("gx", "gy")
    pair = P(None, "gx", "gy")
    return jax.shard_map(
        functools.partial(shards, mesh.shape["gx"], mesh.shape["gy"]),
        mesh=mesh,
        in_specs=(pair, pair, tile, tile, tile, tile, tile, P("gx", None), P("gy", None)),
        out_specs=(pair, tile),
        check_vma=False,
    )
```

```python
import functools

import jax
import jax.numpy as jnp
from jax import lax
from jax.experimental import pallas as pl
from jax.experimental.pallas import tpu as pltpu
from jax.sharding import PartitionSpec as P

SWEEPS = 3
ROWS = 64
LT = 128
VMEM_LIMIT = 48 * 1024 * 1024
MESH = pl.DeviceIdType.MESH
F32 = jnp.float32
BF16 = jnp.bfloat16


def kernel(
    ngx, ngy,
    vel_h, obs_h, thick_h, rate_h, fric_h, mask_h, codes_h, mx_h, my_h,
    adj, coef_ref,
    vel, obs, thick, rate, fric, mask, codes, mx, my,
    s_pad, q1, q2, p_f, g_f, e_f, grad, mxt, myt, t_hi, t_lo,
    edge_out, edge_in, halo, r_send, r_acc, r_in, half_in, z_out, z_in,
    vel_sem, load_sem, halo_send, halo_recv, col_send, col_recv,
    pair_send, pair_recv, half_send, half_recv, z_send, z_recv,
):
    h, w = thick.shape
    nt = w // LT
    ix, iy = lax.axis_index("gx"), lax.axis_index("gy")
    body = pl.ds(8, h)
    outer, inner = (0, nt - 1), tuple(range(1, nt - 1))

    vel_loads = [
        pltpu.make_async_copy(
            vel_h.at[:, :, pl.ds(t * LT, LT)], vel.at[:, t, body], vel_sem.at[t])
        for t in outer + inner
    ]
    loads = [
        pltpu.make_async_copy(thick_h, thick, load_sem.at[0]),
        pltpu.make_async_copy(rate_h, rate, load_sem.at[1]),
        pltpu.make_async_copy(mask_h, mask, load_sem.at[2]),
        pltpu.make_async_copy(fric_h, fric, load_sem.at[3]),
        pltpu.make_async_copy(codes_h, codes, load_sem.at[4]),
        pltpu.make_async_copy(obs_h, obs, load_sem.at[5]),
        pltpu.make_async_copy(mx_h, mx, load_sem.at[6]),
        pltpu.make_async_copy(my_h, my, load_sem.at[7]),
    ]
    for load in vel_loads + loads:
        load.start()

    barrier = pltpu.get_barrier_semaphore()
    for off in range(1, ngx):
        pl.semaphore_signal(barrier, inc=1, device_id=(lax.rem(ix + off, ngx), iy), device_id_type=MESH)
    for off in range(1, ngy):
        pl.semaphore_signal(barrier, inc=1, device_id=(ix, lax.rem(iy + off, ngy)), device_id_type=MESH)
    pl.semaphore_wait(barrier, ngx - 1 + ngy - 1)

    has_n, has_s, has_w, has_e = ix > 0, ix < ngx - 1, iy > 0, iy < ngy - 1

    fields = (vel, s_pad, q1, q2)

    for missing, rows in ((ix == 0, 0), (ix == ngx - 1, h + 8)):

        @pl.when(missing)
        def _(rows=rows):
            for ref in fields:
                ref[:, :, pl.ds(rows, 8)] = jnp.zeros((ref.shape[0], nt, 8, LT), F32)

    for missing, side in ((iy == 0, 0), (iy == ngy - 1, 1)):

        @pl.when(missing)
        def _(side=side):
            edge_in[:, side] = jnp.zeros((4, 8, h), F32)

    def copies_of(k):
        ref = fields[k]
        down = pltpu.make_async_remote_copy(
            ref.at[:, :, pl.ds(h, 8)], ref.at[:, :, pl.ds(0, 8)],
            halo_send.at[k, 0], halo_recv.at[k, 0], device_id=(ix + 1, iy), device_id_type=MESH)
        up = pltpu.make_async_remote_copy(
            ref.at[:, :, pl.ds(8, 8)], ref.at[:, :, pl.ds(h + 8, 8)],
            halo_send.at[k, 1], halo_recv.at[k, 1], device_id=(ix - 1, iy), device_id_type=MESH)
        east = pltpu.make_async_remote_copy(
            edge_out.at[k], edge_in.at[k, 0],
            col_send.at[k, 0], col_recv.at[k, 0], device_id=(ix, iy + 1), device_id_type=MESH)
        west = pltpu.make_async_remote_copy(
            edge_out.at[k], edge_in.at[k, 1],
            col_send.at[k, 1], col_recv.at[k, 1], device_id=(ix, iy - 1), device_id_type=MESH)
        return (has_s, down), (has_n, up), (has_e, east), (has_w, west)

    def start(there, copy):
        @pl.when(there)
        def _():
            copy.start()

    def send_rows(k):
        for there, copy in copies_of(k)[:2]:
            start(there, copy)

    def send_columns(k):
        ref = fields[k]
        lane = lax.broadcasted_iota(jnp.int32, (h, LT), 1)
        pack = pltpu.roll(ref[0, nt - 1, body], 1, 1)
        pack = jnp.where(lane == 7, pltpu.roll(ref[0, 0, body], 7, 1), pack)
        if ref.shape[0] == 2:
            pack = jnp.where(lane == 1, pltpu.roll(ref[1, nt - 1, body], 2, 1), pack)
            pack = jnp.where(lane == 6, pltpu.roll(ref[1, 0, body], 6, 1), pack)
        edge_out[k] = pack.T[:8]
        for there, copy in copies_of(k)[2:]:
            start(there, copy)

    def take_edges(k):
        (_, down), (_, up), (_, east), (_, west) = copies_of(k)
        for there, copy in ((has_w, east), (has_e, west), (has_n, down), (has_s, up)):

            @pl.when(there)
            def _(copy=copy):
                copy.wait_recv()

        row = lax.broadcasted_iota(jnp.int32, (8, h), 0)
        both = jnp.where(row < 4, edge_in[k, 0], edge_in[k, 1])
        halo[k] = jnp.concatenate([both] * (LT // 8), axis=0).T

    def drain_edges(k):
        for there, copy in copies_of(k):

            @pl.when(there)
            def _(copy=copy):
                copy.wait_send()

    def rows_of(step, first, last, stride=ROWS):
        def one(i, carry):
            step(pl.multiple_of(first + i * stride, ROWS))
            return carry

        lax.fori_loop(0, (last - first) // stride, one, 0, unroll=2)

    def border(step):
        rows_of(lambda r: step(r, outer), 0, h)
        rows_of(lambda r: step(r, inner), 0, 2 * (h - ROWS), h - ROWS)

    def interior(step):
        rows_of(lambda r: step(r, inner), ROWS, h - ROWS)

    lanes = lax.broadcasted_iota(jnp.int32, (ROWS, LT), 1)
    at_first, at_last = lanes == 0, lanes == LT - 1

    def cols(t):
        return pl.ds(t * LT, LT)

    def neighbours(k, c, r, t, kept):
        ref = fields[k]

        def turned(tile, by):
            if (c, tile, by) not in kept:
                kept[c, tile, by] = pltpu.roll(ref[c, tile, pl.ds(r + 8, ROWS)], by, 1)
            return kept[c, tile, by]

        def edge(by):
            value = halo[k, pl.ds(r, ROWS)]
            return pltpu.roll(value, by, 1) if c else value

        up = ref[c, t, pl.ds(r + 7, ROWS)]
        down = ref[c, t, pl.ds(r + 9, ROWS)]
        before = turned(t - 1, 1) if t else edge(LT - 1)
        after = turned(t + 1, LT - 1) if t < nt - 1 else edge(1)
        left = jnp.where(at_first, before, turned(t, 1))
        right = jnp.where(at_last, after, turned(t, LT - 1))
        return up, down, left, right

    def weighted(k, c, r, t, kept):
        up, down, left, right = neighbours(k, c, r, t, kept)
        ns, ew = up + down, left + right
        return 4.0 * ns + ew if c == 0 else ns + 4.0 * ew

    def viscosity(r, tiles):
        kept = {}
        for t in tiles:
            up, down, left, right = neighbours(0, 0, r, t, kept)
            ux, uy = down - up, right - left
            up, down, left, right = neighbours(0, 1, r, t, kept)
            vx, vy = down - up, right - left
            shear = uy + vx
            strain = 0.25 * (ux * ux + vy * vy + ux * vy + 0.25 * (shear * shear))
            here = pl.ds(r, ROWS)
            half = 0.5 * thick[here, cols(t)] * rate[here, cols(t)]
            root = half * lax.rsqrt(half) * jnp.exp2(jnp.log2(strain + 0.01) * (-1.0 / 6.0))
            s_pad[0, t, pl.ds(r + 8, ROWS)] = jnp.where(mask[here, cols(t)] >= 1, root, 0.0)

    def sources(r, tiles):
        here, there = pl.ds(r, ROWS), pl.ds(r + 8, ROWS)
        for t in tiles:
            kind = mask[here, cols(t)]
            s = s_pad[0, t, there]
            drag = jnp.where(kind == 2, fric[here, cols(t)], 0.0)
            fric[here, cols(t)] = drag
            code = codes[here, cols(t)] & 15
            pairs = code - (lax.shift_right_logical(code, 1) & 5)
            fronts = ((pairs & 3) + lax.shift_right_logical(pairs, 2)).astype(F32)
            e_f[here, cols(t)] = 2.0 * (s * s) * fronts + drag + 1.0
            for c in range(2):
                obs[c, here, cols(t)] = jnp.where(kind >= 1, vel[c, t, there] - obs[c, here, cols(t)], 0.0)

    def first(r, tiles):
        here, there = pl.ds(r, ROWS), pl.ds(r + 8, ROWS)
        kept = {}
        for t in tiles:
            up, down, left, right = neighbours(1, 0, r, t, kept)
            ns, ew = up + down, left + right
            s = s_pad[0, t, there]
            e = e_f[here, cols(t)]
            for c, total in ((0, 4.0 * ns + ew), (1, ns + 4.0 * ew)):
                inverse = 1.0 / (s * total + e)
                value = obs[c, here, cols(t)] * inverse
                p_f[c, here, cols(t)] = value
                g_f[c, here, cols(t)] = s * inverse
                q1[c, t, there] = s * value

    def second(r, tiles):
        here, there = pl.ds(r, ROWS), pl.ds(r + 8, ROWS)
        kept = {}
        for t in tiles:
            s = s_pad[0, t, there]
            for c in range(2):
                total = weighted(2, c, r, t, kept)
                q2[c, t, there] = q1[c, t, there] + s * g_f[c, here, cols(t)] * total

    def third(r, tiles):
        here, there = pl.ds(r, ROWS), pl.ds(r + 8, ROWS)
        kept = {}
        for t in tiles:
            flux = None
            for c in range(2):
                value = p_f[c, here, cols(t)] + g_f[c, here, cols(t)] * weighted(3, c, r, t, kept)
                adj[c, here, cols(t)] = value
                term = vel[c, t, there] * value
                flux = term if flux is None else flux + term
            grad[here, cols(t)] = (-fric[here, cols(t)] * flux).astype(BF16)

    for load in vel_loads:
        load.wait()
    send_rows(0)
    send_columns(0)
    for load in loads[:3]:
        load.wait()
    take_edges(0)
    border(viscosity)
    send_columns(1)
    send_rows(1)
    interior(viscosity)
    for load in loads[3:]:
        load.wait()
    rows_of(lambda r: sources(r, range(nt)), 0, h)
    mxt[...] = mx[...].T
    myt[...] = my[...].T.reshape(myt.shape)
    take_edges(1)
    border(first)
    send_columns(2)
    send_rows(2)
    interior(first)
    take_edges(2)
    border(second)
    send_columns(3)
    send_rows(3)
    interior(second)
    interior(third)
    take_edges(3)
    border(third)

    nblk, kb, km = r_acc.shape
    npc, ab = km // LT, km // ngx
    core = lax.rem(iy, 2)
    cell = iy // 2
    nbits = nblk.bit_length() - 1
    bits = [lax.rem(cell // (1 << t), 2) for t in range(nbits)]
    rows_dims = (((1,), (1,)), ((), ()))
    sent = []

    def project(side, p):
        rows = myt[:, side].reshape(nblk * kb, w)
        out = lax.dot_general(rows, t_hi[p], rows_dims, preferred_element_type=F32)
        out = out + lax.dot_general(rows, t_lo[p], rows_dims, preferred_element_type=F32)
        return out.reshape(nblk, kb, LT)

    pairs = []
    for p in range(npc):
        table = jnp.dot(mxt[p * LT : (p + 1) * LT, :], grad[...], preferred_element_type=F32)
        high = table.astype(BF16)
        t_hi[p] = high
        t_lo[p] = (table - high.astype(F32)).astype(BF16)
        r_send[p] = project(1 - core, p)
        pair = pltpu.make_async_remote_copy(
            r_send.at[p], r_in.at[p], pair_send.at[p], pair_recv.at[p],
            device_id=(ix, iy + 1 - 2 * core), device_id_type=MESH)
        pair.start()
        pairs.append(pair)
    for p in range(npc):
        r_acc[:, :, p * LT : (p + 1) * LT] = project(core, p)

    live = [[] for _ in range(npc)]
    flying = [[] for _ in range(npc)]
    slot = 0
    for stage in range(nbits + 1):
        for p in range(npc):
            lanes = pl.ds(p * LT, LT)
            if stage == 0:
                pairs[p].wait_recv()
                r_acc[:, :, lanes] += r_in[p]
                sent.append(pairs[p])
            for copy, dst, place in flying[p]:
                copy.wait_recv()
                r_acc[dst, :, lanes] += half_in[place]
                sent.append(copy)
            flying[p] = []
            if stage < nbits:
                t = nbits - 1 - stage if p % 2 else stage
                free = [b for b in range(nbits) if b not in live[p] and b != t]
                for combo in range(1 << len(free)):
                    fixed = sum(((combo >> n) & 1) << b for n, b in enumerate(free))
                    fixed = fixed + sum((bits[b] * (1 << b) for b in live[p]), 0)
                    src = fixed + (1 - bits[t]) * (1 << t)
                    dst = fixed + bits[t] * (1 << t)
                    copy = pltpu.make_async_remote_copy(
                        r_acc.at[src, :, lanes], half_in.at[slot],
                        half_send.at[slot], half_recv.at[slot],
                        device_id=(ix, iy + (1 - 2 * bits[t]) * (2 << t)), device_id_type=MESH)
                    copy.start()
                    flying[p].append((copy, dst, slot))
                    slot += 1
                live[p].append(t)
            else:
                for d in range(p * LT // ab, (p + 1) * LT // ab):
                    z_out[d] = r_acc[cell, :, d * ab : (d + 1) * ab]

                    @pl.when(ix != d)
                    def _(d=d):
                        pltpu.make_async_remote_copy(
                            z_out.at[d], z_in.at[ix], z_send.at[d], z_recv.at[ix],
                            device_id=(d, iy), device_id_type=MESH).start()

    def z_copy(d):
        return pltpu.make_async_remote_copy(
            z_out.at[d], z_in.at[d], z_send.at[d], z_recv.at[d],
            device_id=(d, iy), device_id_type=MESH)

    coef_ref[...] = z_out[ix]
    for d in range(ngx):

        @pl.when(ix != d)
        def _(d=d):
            z_copy(d).wait_recv()
            coef_ref[...] += z_in[d]

    for d in range(ngx):

        @pl.when(ix != d)
        def _(d=d):
            z_copy(d).wait_send()

    for copy in sent:
        copy.wait_send()
    for k in range(4):
        drain_edges(k)


def write_results(adj, coef, adj_h, coef_h, adj_sem, coef_sem):
    rows = adj.shape[1] // 2
    copies = [pltpu.make_async_copy(coef, coef_h, coef_sem)]
    for n in range(4):
        part = (n % 2, pl.ds(n // 2 * rows, rows))
        copies.append(pltpu.make_async_copy(adj.at[part], adj_h.at[part], adj_sem.at[n]))
    for copy in copies:
        copy.start()
    for copy in copies:
        copy.wait()


def shards(ngx, ngy, velocity, observed, thickness, rate_factor, friction, cell_mask, front_codes, modes_x, modes_y):
    h, w = thickness.shape
    km = modes_x.shape[1]
    nblk, kb, ab = ngy // 2, km // ngy, km // ngx
    npc = km // LT
    slots = npc * sum(nblk >> (t + 1) for t in range(nblk.bit_length() - 1))
    hbm_spec = pl.BlockSpec(memory_space=pltpu.HBM)
    vmem_spec = pl.BlockSpec(memory_space=pltpu.VMEM)
    pad = (w // LT, h + 16, LT)
    dma = pltpu.SemaphoreType.DMA
    args = (velocity, observed, thickness, rate_factor, friction, cell_mask, front_codes, modes_x, modes_y)
    args = [pltpu.with_memory_space_constraint(x, pltpu.HBM) for x in args]
    adjoint, coefficients = pl.pallas_call(
        functools.partial(kernel, ngx, ngy),
        out_shape=(pltpu.VMEM((2, h, w), F32), pltpu.VMEM((kb, ab), F32)),
        in_specs=[hbm_spec] * 9,
        out_specs=(vmem_spec, vmem_spec),
        scratch_shapes=[
            pltpu.VMEM((2, *pad), F32),
            pltpu.VMEM((2, h, w), F32),
            pltpu.VMEM((h, w), F32),
            pltpu.VMEM((h, w), F32),
            pltpu.VMEM((h, w), F32),
            pltpu.VMEM((h, w), jnp.int32),
            pltpu.VMEM((h, w), jnp.int32),
            pltpu.VMEM((h, km), BF16),
            pltpu.VMEM((w, km), BF16),
            pltpu.VMEM((1, *pad), F32),
            pltpu.VMEM((2, *pad), F32),
            pltpu.VMEM((2, *pad), F32),
            pltpu.VMEM((2, h, w), F32),
            pltpu.VMEM((2, h, w), F32),
            pltpu.VMEM((h, w), F32),
            pltpu.VMEM((h, w), BF16),
            pltpu.VMEM((km, h), BF16),
            pltpu.VMEM((nblk, 2, kb, w), BF16),
            pltpu.VMEM((npc, LT, w), BF16),
            pltpu.VMEM((npc, LT, w), BF16),
            pltpu.VMEM((4, 8, h), F32),
            pltpu.VMEM((4, 2, 8, h), F32),
            pltpu.VMEM((4, h, LT), F32),
            pltpu.VMEM((npc, nblk, kb, LT), F32),
            pltpu.VMEM((nblk, kb, km), F32),
            pltpu.VMEM((npc, nblk, kb, LT), F32),
            pltpu.VMEM((slots, kb, LT), F32),
            pltpu.VMEM((ngx, kb, ab), F32),
            pltpu.VMEM((ngx, kb, ab), F32),
            dma((w // LT,)),
            dma((8,)),
            dma((4, 2)),
            dma((4, 2)),
            dma((4, 2)),
            dma((4, 2)),
            dma((npc,)),
            dma((npc,)),
            dma((slots,)),
            dma((slots,)),
            dma((ngx,)),
            dma((ngx,)),
        ],
        compiler_params=pltpu.CompilerParams(
            collective_id=0, has_side_effects=True, vmem_limit_bytes=VMEM_LIMIT
        ),
    )(*args)
    adjoint = pltpu.with_memory_space_constraint(adjoint, pltpu.VMEM)
    coefficients = pltpu.with_memory_space_constraint(coefficients, pltpu.VMEM)
    adjoint, coefficients = pl.pallas_call(
        write_results,
        out_shape=(
            jax.ShapeDtypeStruct((2, h, w), F32),
            jax.ShapeDtypeStruct((kb, ab), F32),
        ),
        in_specs=[vmem_spec, vmem_spec],
        out_specs=(hbm_spec, hbm_spec),
        scratch_shapes=[dma((4,)), dma],
    )(adjoint, coefficients)
    return adjoint, coefficients.T


def solution(mesh):
    tile = P("gx", "gy")
    pair = P(None, "gx", "gy")
    return jax.shard_map(
        functools.partial(shards, mesh.shape["gx"], mesh.shape["gy"]),
        mesh=mesh,
        in_specs=(pair, pair, tile, tile, tile, tile, tile, P("gx", None), P("gy", None)),
        out_specs=(pair, tile),
        check_vma=False,
    )
```

```python
import functools

import jax
import jax.numpy as jnp
from jax import lax
from jax.experimental import pallas as pl
from jax.experimental.pallas import tpu as pltpu
from jax.sharding import PartitionSpec as P

SWEEPS = 3
ROWS = 64
LT = 128
VMEM_LIMIT = 48 * 1024 * 1024
MESH = pl.DeviceIdType.MESH
F32 = jnp.float32
BF16 = jnp.bfloat16


def kernel(
    ngx, ngy,
    vel_h, obs_h, thick_h, rate_h, fric_h, mask_h, codes_h, mx_h, my_h,
    adj, coef_ref,
    vel, obs, thick, rate, fric, mask, codes, mx, my,
    s_pad, q1, q2, p_f, g_f, e_f, grad, mxt, myt, t_hi, t_lo,
    edge_out, edge_in, halo, r_send, r_acc, r_in, half_in, z_out, z_in,
    vel_sem, load_sem, halo_send, halo_recv, col_send, col_recv,
    pair_send, pair_recv, half_send, half_recv, z_send, z_recv,
):
    h, w = thick.shape
    nt = w // LT
    ix, iy = lax.axis_index("gx"), lax.axis_index("gy")
    body = pl.ds(8, h)
    outer, inner = (0, nt - 1), tuple(range(1, nt - 1))

    vel_loads = [
        pltpu.make_async_copy(
            vel_h.at[:, :, pl.ds(t * LT, LT)], vel.at[:, t, body], vel_sem.at[t])
        for t in outer + inner
    ]
    loads = [
        pltpu.make_async_copy(thick_h, thick, load_sem.at[0]),
        pltpu.make_async_copy(rate_h, rate, load_sem.at[1]),
        pltpu.make_async_copy(mask_h, mask, load_sem.at[2]),
        pltpu.make_async_copy(fric_h, fric, load_sem.at[3]),
        pltpu.make_async_copy(codes_h, codes, load_sem.at[4]),
        pltpu.make_async_copy(obs_h, obs, load_sem.at[5]),
        pltpu.make_async_copy(mx_h, mx, load_sem.at[6]),
        pltpu.make_async_copy(my_h, my, load_sem.at[7]),
    ]
    for load in vel_loads + loads:
        load.start()

    barrier = pltpu.get_barrier_semaphore()
    for off in range(1, ngx):
        pl.semaphore_signal(barrier, inc=1, device_id=(lax.rem(ix + off, ngx), iy), device_id_type=MESH)
    for off in range(1, ngy):
        pl.semaphore_signal(barrier, inc=1, device_id=(ix, lax.rem(iy + off, ngy)), device_id_type=MESH)
    pl.semaphore_wait(barrier, ngx - 1 + ngy - 1)

    has_n, has_s, has_w, has_e = ix > 0, ix < ngx - 1, iy > 0, iy < ngy - 1

    fields = (vel, s_pad, q1, q2)

    for missing, rows in ((ix == 0, 0), (ix == ngx - 1, h + 8)):

        @pl.when(missing)
        def _(rows=rows):
            for ref in fields:
                ref[:, :, pl.ds(rows, 8)] = jnp.zeros((ref.shape[0], nt, 8, LT), F32)

    for missing, side in ((iy == 0, 0), (iy == ngy - 1, 1)):

        @pl.when(missing)
        def _(side=side):
            edge_in[:, side] = jnp.zeros((4, 8, h), F32)

    def copies_of(k):
        ref = fields[k]
        down = pltpu.make_async_remote_copy(
            ref.at[:, :, pl.ds(h, 8)], ref.at[:, :, pl.ds(0, 8)],
            halo_send.at[k, 0], halo_recv.at[k, 0], device_id=(ix + 1, iy), device_id_type=MESH)
        up = pltpu.make_async_remote_copy(
            ref.at[:, :, pl.ds(8, 8)], ref.at[:, :, pl.ds(h + 8, 8)],
            halo_send.at[k, 1], halo_recv.at[k, 1], device_id=(ix - 1, iy), device_id_type=MESH)
        east = pltpu.make_async_remote_copy(
            edge_out.at[k], edge_in.at[k, 0],
            col_send.at[k, 0], col_recv.at[k, 0], device_id=(ix, iy + 1), device_id_type=MESH)
        west = pltpu.make_async_remote_copy(
            edge_out.at[k], edge_in.at[k, 1],
            col_send.at[k, 1], col_recv.at[k, 1], device_id=(ix, iy - 1), device_id_type=MESH)
        return (has_s, down), (has_n, up), (has_e, east), (has_w, west)

    def start(there, copy):
        @pl.when(there)
        def _():
            copy.start()

    def send_rows(k):
        for there, copy in copies_of(k)[:2]:
            start(there, copy)

    def send_columns(k):
        ref = fields[k]
        lane = lax.broadcasted_iota(jnp.int32, (h, LT), 1)
        pack = pltpu.roll(ref[0, nt - 1, body], 1, 1)
        pack = jnp.where(lane == 7, pltpu.roll(ref[0, 0, body], 7, 1), pack)
        if ref.shape[0] == 2:
            pack = jnp.where(lane == 1, pltpu.roll(ref[1, nt - 1, body], 2, 1), pack)
            pack = jnp.where(lane == 6, pltpu.roll(ref[1, 0, body], 6, 1), pack)
        edge_out[k] = pack.T[:8]
        for there, copy in copies_of(k)[2:]:
            start(there, copy)

    def take_edges(k):
        (_, down), (_, up), (_, east), (_, west) = copies_of(k)
        for there, copy in ((has_w, east), (has_e, west), (has_n, down), (has_s, up)):

            @pl.when(there)
            def _(copy=copy):
                copy.wait_recv()

        row = lax.broadcasted_iota(jnp.int32, (8, h), 0)
        both = jnp.where(row < 4, edge_in[k, 0], edge_in[k, 1])
        halo[k] = jnp.concatenate([both] * (LT // 8), axis=0).T

    def drain_edges(k):
        for there, copy in copies_of(k):

            @pl.when(there)
            def _(copy=copy):
                copy.wait_send()

    def rows_of(step, first, last, stride=ROWS):
        def one(i, carry):
            step(pl.multiple_of(first + i * stride, ROWS))
            return carry

        lax.fori_loop(0, (last - first) // stride, one, 0, unroll=2)

    def border(step):
        rows_of(lambda r: step(r, outer), 0, h)
        rows_of(lambda r: step(r, inner), 0, 2 * (h - ROWS), h - ROWS)

    def interior(step):
        rows_of(lambda r: step(r, inner), ROWS, h - ROWS)

    lanes = lax.broadcasted_iota(jnp.int32, (ROWS, LT), 1)
    at_first, at_last = lanes == 0, lanes == LT - 1

    def cols(t):
        return pl.ds(t * LT, LT)

    def neighbours(k, c, r, t, kept):
        ref = fields[k]

        def turned(tile, by):
            if (c, tile, by) not in kept:
                kept[c, tile, by] = pltpu.roll(ref[c, tile, pl.ds(r + 8, ROWS)], by, 1)
            return kept[c, tile, by]

        def edge(by):
            value = halo[k, pl.ds(r, ROWS)]
            return pltpu.roll(value, by, 1) if c else value

        up = ref[c, t, pl.ds(r + 7, ROWS)]
        down = ref[c, t, pl.ds(r + 9, ROWS)]
        before = turned(t - 1, 1) if t else edge(LT - 1)
        after = turned(t + 1, LT - 1) if t < nt - 1 else edge(1)
        left = jnp.where(at_first, before, turned(t, 1))
        right = jnp.where(at_last, after, turned(t, LT - 1))
        return up, down, left, right

    def weighted(k, c, r, t, kept):
        up, down, left, right = neighbours(k, c, r, t, kept)
        ns, ew = up + down, left + right
        return 4.0 * ns + ew if c == 0 else ns + 4.0 * ew

    def viscosity(r, tiles):
        kept = {}
        for t in tiles:
            up, down, left, right = neighbours(0, 0, r, t, kept)
            ux, uy = down - up, right - left
            up, down, left, right = neighbours(0, 1, r, t, kept)
            vx, vy = down - up, right - left
            shear = uy + vx
            strain = 0.25 * (ux * ux + vy * vy + ux * vy + 0.25 * (shear * shear))
            here = pl.ds(r, ROWS)
            half = 0.5 * thick[here, cols(t)] * rate[here, cols(t)]
            root = half * lax.rsqrt(half) * jnp.exp2(jnp.log2(strain + 0.01) * (-1.0 / 6.0))
            s_pad[0, t, pl.ds(r + 8, ROWS)] = jnp.where(mask[here, cols(t)] >= 1, root, 0.0)

    def sources(r, tiles):
        here, there = pl.ds(r, ROWS), pl.ds(r + 8, ROWS)
        for t in tiles:
            kind = mask[here, cols(t)]
            s = s_pad[0, t, there]
            drag = jnp.where(kind == 2, fric[here, cols(t)], 0.0)
            fric[here, cols(t)] = drag
            code = codes[here, cols(t)] & 15
            pairs = code - (lax.shift_right_logical(code, 1) & 5)
            fronts = ((pairs & 3) + lax.shift_right_logical(pairs, 2)).astype(F32)
            e_f[here, cols(t)] = 2.0 * (s * s) * fronts + drag + 1.0
            for c in range(2):
                obs[c, here, cols(t)] = jnp.where(kind >= 1, vel[c, t, there] - obs[c, here, cols(t)], 0.0)

    def first(r, tiles):
        here, there = pl.ds(r, ROWS), pl.ds(r + 8, ROWS)
        kept = {}
        for t in tiles:
            up, down, left, right = neighbours(1, 0, r, t, kept)
            ns, ew = up + down, left + right
            s = s_pad[0, t, there]
            e = e_f[here, cols(t)]
            for c, total in ((0, 4.0 * ns + ew), (1, ns + 4.0 * ew)):
                inverse = 1.0 / (s * total + e)
                value = obs[c, here, cols(t)] * inverse
                p_f[c, here, cols(t)] = value
                g_f[c, here, cols(t)] = s * inverse
                q1[c, t, there] = s * value

    def second(r, tiles):
        here, there = pl.ds(r, ROWS), pl.ds(r + 8, ROWS)
        kept = {}
        for t in tiles:
            s = s_pad[0, t, there]
            for c in range(2):
                total = weighted(2, c, r, t, kept)
                q2[c, t, there] = q1[c, t, there] + s * g_f[c, here, cols(t)] * total

    def third(r, tiles):
        here, there = pl.ds(r, ROWS), pl.ds(r + 8, ROWS)
        kept = {}
        for t in tiles:
            flux = None
            for c in range(2):
                value = p_f[c, here, cols(t)] + g_f[c, here, cols(t)] * weighted(3, c, r, t, kept)
                adj[c, here, cols(t)] = value
                term = vel[c, t, there] * value
                flux = term if flux is None else flux + term
            grad[here, cols(t)] = (-fric[here, cols(t)] * flux).astype(BF16)

    for load in vel_loads:
        load.wait()
    send_rows(0)
    send_columns(0)
    for load in loads[:3]:
        load.wait()
    take_edges(0)
    border(viscosity)
    send_columns(1)
    send_rows(1)
    interior(viscosity)
    for load in loads[3:]:
        load.wait()
    rows_of(lambda r: sources(r, range(nt)), 0, h)
    mxt[...] = mx[...].T
    myt[...] = my[...].T.reshape(myt.shape)
    take_edges(1)
    border(first)
    send_columns(2)
    send_rows(2)
    interior(first)
    take_edges(2)
    border(second)
    send_columns(3)
    send_rows(3)
    interior(second)
    interior(third)
    take_edges(3)
    border(third)

    npc, nblk, kb, _ = r_acc.shape
    ab = npc * LT // ngx
    core = lax.rem(iy, 2)
    cell = iy // 2
    nbits = nblk.bit_length() - 1
    bits = [lax.rem(cell // (1 << t), 2) for t in range(nbits)]
    rows_dims = (((1,), (1,)), ((), ()))
    sent = []

    def project(side, p):
        rows = myt[:, side].reshape(nblk * kb, w)
        out = lax.dot_general(rows, t_hi[p], rows_dims, preferred_element_type=F32)
        out = out + lax.dot_general(rows, t_lo[p], rows_dims, preferred_element_type=F32)
        return out.reshape(nblk, kb, LT)

    pairs = []
    for p in range(npc):
        table = jnp.dot(mxt[p * LT : (p + 1) * LT, :], grad[...], preferred_element_type=F32)
        high = table.astype(BF16)
        t_hi[p] = high
        t_lo[p] = (table - high.astype(F32)).astype(BF16)
        r_send[p] = project(1 - core, p)
        pair = pltpu.make_async_remote_copy(
            r_send.at[p], r_in.at[p], pair_send.at[p], pair_recv.at[p],
            device_id=(ix, iy + 1 - 2 * core), device_id_type=MESH)
        pair.start()
        pairs.append(pair)

    live = [[] for _ in range(npc)]
    flying = [[] for _ in range(npc)]
    slot = 0
    for stage in range(nbits + 1):
        for p in range(npc):
            if stage == 0:
                r_acc[p] = project(core, p)
                pairs[p].wait_recv()
                r_acc[p] += r_in[p]
                sent.append(pairs[p])
            for copy, dst, place in flying[p]:
                copy.wait_recv()
                r_acc[p, dst] += half_in[place]
                sent.append(copy)
            flying[p] = []
            if stage < nbits:
                t = nbits - 1 - stage if p % 2 else stage
                free = [b for b in range(nbits) if b not in live[p] and b != t]
                for combo in range(1 << len(free)):
                    fixed = sum(((combo >> n) & 1) << b for n, b in enumerate(free))
                    fixed = fixed + sum((bits[b] * (1 << b) for b in live[p]), 0)
                    src = fixed + (1 - bits[t]) * (1 << t)
                    dst = fixed + bits[t] * (1 << t)
                    copy = pltpu.make_async_remote_copy(
                        r_acc.at[p, src], half_in.at[slot],
                        half_send.at[slot], half_recv.at[slot],
                        device_id=(ix, iy + (1 - 2 * bits[t]) * (2 << t)), device_id_type=MESH)
                    copy.start()
                    flying[p].append((copy, dst, slot))
                    slot += 1
                live[p].append(t)
            else:
                for d in range(p * LT // ab, (p + 1) * LT // ab):
                    z_out[d] = r_acc[p, cell, :, d * ab - p * LT : (d + 1) * ab - p * LT]

                    @pl.when(ix != d)
                    def _(d=d):
                        pltpu.make_async_remote_copy(
                            z_out.at[d], z_in.at[ix], z_send.at[d], z_recv.at[ix],
                            device_id=(d, iy), device_id_type=MESH).start()

    def z_copy(d):
        return pltpu.make_async_remote_copy(
            z_out.at[d], z_in.at[d], z_send.at[d], z_recv.at[d],
            device_id=(d, iy), device_id_type=MESH)

    coef_ref[...] = z_out[ix]
    for d in range(ngx):

        @pl.when(ix != d)
        def _(d=d):
            z_copy(d).wait_recv()
            coef_ref[...] += z_in[d]

    for d in range(ngx):

        @pl.when(ix != d)
        def _(d=d):
            z_copy(d).wait_send()

    for copy in sent:
        copy.wait_send()
    for k in range(4):
        drain_edges(k)


def write_results(adj, coef, adj_h, coef_h, adj_sem, coef_sem):
    rows = adj.shape[1] // 2
    copies = [pltpu.make_async_copy(coef, coef_h, coef_sem)]
    for n in range(4):
        part = (n % 2, pl.ds(n // 2 * rows, rows))
        copies.append(pltpu.make_async_copy(adj.at[part], adj_h.at[part], adj_sem.at[n]))
    for copy in copies:
        copy.start()
    for copy in copies:
        copy.wait()


def shards(ngx, ngy, velocity, observed, thickness, rate_factor, friction, cell_mask, front_codes, modes_x, modes_y):
    h, w = thickness.shape
    km = modes_x.shape[1]
    nblk, kb, ab = ngy // 2, km // ngy, km // ngx
    npc = km // LT
    slots = npc * sum(nblk >> (t + 1) for t in range(nblk.bit_length() - 1))
    hbm_spec = pl.BlockSpec(memory_space=pltpu.HBM)
    vmem_spec = pl.BlockSpec(memory_space=pltpu.VMEM)
    pad = (w // LT, h + 16, LT)
    dma = pltpu.SemaphoreType.DMA
    args = (velocity, observed, thickness, rate_factor, friction, cell_mask, front_codes, modes_x, modes_y)
    args = [pltpu.with_memory_space_constraint(x, pltpu.HBM) for x in args]
    adjoint, coefficients = pl.pallas_call(
        functools.partial(kernel, ngx, ngy),
        out_shape=(pltpu.VMEM((2, h, w), F32), pltpu.VMEM((kb, ab), F32)),
        in_specs=[hbm_spec] * 9,
        out_specs=(vmem_spec, vmem_spec),
        scratch_shapes=[
            pltpu.VMEM((2, *pad), F32),
            pltpu.VMEM((2, h, w), F32),
            pltpu.VMEM((h, w), F32),
            pltpu.VMEM((h, w), F32),
            pltpu.VMEM((h, w), F32),
            pltpu.VMEM((h, w), jnp.int32),
            pltpu.VMEM((h, w), jnp.int32),
            pltpu.VMEM((h, km), BF16),
            pltpu.VMEM((w, km), BF16),
            pltpu.VMEM((1, *pad), F32),
            pltpu.VMEM((2, *pad), F32),
            pltpu.VMEM((2, *pad), F32),
            pltpu.VMEM((2, h, w), F32),
            pltpu.VMEM((2, h, w), F32),
            pltpu.VMEM((h, w), F32),
            pltpu.VMEM((h, w), BF16),
            pltpu.VMEM((km, h), BF16),
            pltpu.VMEM((nblk, 2, kb, w), BF16),
            pltpu.VMEM((npc, LT, w), BF16),
            pltpu.VMEM((npc, LT, w), BF16),
            pltpu.VMEM((4, 8, h), F32),
            pltpu.VMEM((4, 2, 8, h), F32),
            pltpu.VMEM((4, h, LT), F32),
            pltpu.VMEM((npc, nblk, kb, LT), F32),
            pltpu.VMEM((npc, nblk, kb, LT), F32),
            pltpu.VMEM((npc, nblk, kb, LT), F32),
            pltpu.VMEM((slots, kb, LT), F32),
            pltpu.VMEM((ngx, kb, ab), F32),
            pltpu.VMEM((ngx, kb, ab), F32),
            dma((w // LT,)),
            dma((8,)),
            dma((4, 2)),
            dma((4, 2)),
            dma((4, 2)),
            dma((4, 2)),
            dma((npc,)),
            dma((npc,)),
            dma((slots,)),
            dma((slots,)),
            dma((ngx,)),
            dma((ngx,)),
        ],
        compiler_params=pltpu.CompilerParams(
            collective_id=0, has_side_effects=True, vmem_limit_bytes=VMEM_LIMIT
        ),
    )(*args)
    adjoint = pltpu.with_memory_space_constraint(adjoint, pltpu.VMEM)
    coefficients = pltpu.with_memory_space_constraint(coefficients, pltpu.VMEM)
    adjoint, coefficients = pl.pallas_call(
        write_results,
        out_shape=(
            jax.ShapeDtypeStruct((2, h, w), F32),
            jax.ShapeDtypeStruct((kb, ab), F32),
        ),
        in_specs=[vmem_spec, vmem_spec],
        out_specs=(hbm_spec, hbm_spec),
        scratch_shapes=[dma((4,)), dma],
    )(adjoint, coefficients)
    return adjoint, coefficients.T


def solution(mesh):
    tile = P("gx", "gy")
    pair = P(None, "gx", "gy")
    return jax.shard_map(
        functools.partial(shards, mesh.shape["gx"], mesh.shape["gy"]),
        mesh=mesh,
        in_specs=(pair, pair, tile, tile, tile, tile, tile, P("gx", None), P("gy", None)),
        out_specs=(pair, tile),
        check_vma=False,
    )
```
